32 devices in a mesh: grp: 2 (over y), space: 4 (over z), lev: 2 (over x), rk: 2 (over core).
Axes of the slice: x: 2, y: 2, z: 4, core: 2. Of those that a mesh axis runs over, the one named last changes fastest.
Arguments:
- anomaly: bfloat16 [64, 128, 16, 256], P(('grp', 'space'), None, 'lev'), parts along dimension 0, may hold values from -5 to 5
- depth: int32 [64, 128], P(('grp', 'space')), parts along dimension 0, may hold values from 0 to 16
- cell_weight: float32 [64, 128], P(('grp', 'space')), parts along dimension 0, may hold values from 0.5 to 4
- test_matrix: bfloat16 [256, 32], P(None, 'rk'), may hold values from -6 to 6
Outputs:
- eof: float32 [64, 128, 16, 32], P(('grp', 'space'), None, 'lev', 'rk'), parts along dimension 0
- coefficients: float32 [64, 256], P(('grp', 'rk')), parts along dimension 0
The draws below stay inside these ranges and needn't reach their ends.
There are 2 independent parts, one for each index of `grp`. The reference program is written for one: setup_inputs(seed, part) draws one part's arguments, and reference() takes and returns one part's arrays. A program takes and returns all parts, laid end to end along the dimension named above; an argument that names none is the same for every part. Nothing has to cross between parts.
All inputs are finite; a program needn't handle non-finite values.
Results may differ from the reference program's by a relative error of at most 0.0029.
Values may be sent and summed in bfloat16 or wider, within the bound.
A program may use at most 64 MiB of HBM per device.

```python
import math
import jax
import jax.numpy as jnp
import numpy as np
from jax import lax

CB = 128
NT = 256
R = 32
NB = 32
L = 16


def draw_anomaly(key, part):
    key = jax.random.fold_in(key, 7)
    row_key, time_key, noise_key = jax.random.split(key, 3)
    modes = 2 * R
    total_rows = NB * CB * L
    loadings = jax.random.normal(row_key, (total_rows, modes), jnp.float32)
    series = jax.random.normal(time_key, (modes, NT), jnp.float32)
    noise = jax.random.normal(noise_key, (total_rows, NT), jnp.float32)
    steepness = 1.0
    column_scale = jnp.ones((NB * CB, 1, 1), jnp.float32)
    table = (1.0 + np.arange(modes) / (R // 2)) ** (-steepness)
    noise_level = math.sqrt(0.004 * NT)
    normalizer = math.sqrt(float(np.sum(table * table)) + noise_level * noise_level)
    amplitude = jnp.asarray(table, dtype=jnp.float32)
    signal = jnp.dot(loadings * amplitude[None, :], series, precision=lax.Precision.HIGHEST)
    field = (signal + noise_level * noise) / normalizer
    field = field.reshape(NB * CB, L, NT) * column_scale
    return jnp.clip(field, -5.0, 5.0).reshape(NB, CB, L, NT).astype(jnp.bfloat16)


def with_ends(array, rng, least, top_value):
    index_at = [jax.random.randint(jax.random.fold_in(rng, axis), (), 0, length) for axis, length in enumerate(array.shape)]
    main_axis = array.shape.index(max(array.shape))
    beside = index_at[:main_axis] + [(index_at[main_axis] + 1) % array.shape[main_axis]] + index_at[main_axis + 1:]
    return array.at[tuple(index_at)].set(least).at[tuple(beside)].set(top_value)


def block_levels(stream_key, extent, cuts, least, top_value):
    factor_of, own = 1.0, jax.random.fold_in(stream_key, 6)
    for dim, parts in cuts:
        heights = jnp.exp(jax.random.uniform(jax.random.fold_in(own, dim), (parts,), jnp.float32, least / len(cuts), top_value / len(cuts)))
        factor_of = factor_of * jnp.repeat(heights, extent[dim] // parts).reshape([-1 if axis == dim else 1 for axis in range(len(extent))])
    return factor_of


def gaussian(rng, dims, scale, limit, shards=(), held_as=jnp.bfloat16):
    entries = scale * jax.random.normal(rng, dims, jnp.float32)
    if shards:
        entries = entries * block_levels(rng, dims, shards, -0.22, 0.18)
    return jnp.clip(entries, -limit, limit).astype(held_as)


def setup_inputs(seed: int = 0, part: int = 0) -> dict:
    key_list = jax.random.split(jax.random.key(seed), 5)
    part_keys = jax.random.split(jax.random.fold_in(key_list[4], part), 5)
    anomaly = draw_anomaly(jax.random.fold_in(jax.random.fold_in(key_list[4], part), 71), part)
    depth = with_ends(jax.random.randint(part_keys[1], (NB, CB), 0, L + 1), jax.random.fold_in(part_keys[1], 1), 0, L).astype(jnp.int32)
    cell_weight = jnp.clip(jnp.exp(math.log(4.0) - 2.0794415 * jax.random.uniform(part_keys[2], (NB, CB), jnp.float32) ** block_levels(part_keys[2], (NB, CB), ((0, 4),), -0.2, 0.2)), 0.5, 4.0)
    test_matrix = gaussian(key_list[3], (NT, R), 1.0, 6.0, ((1, 2),))
    return {"anomaly": anomaly, "depth": depth, "cell_weight": cell_weight, "test_matrix": test_matrix}


HIGH = lax.Precision.HIGHEST
CONTRACT_ROWS = (((0,), (0,)), ((), ()))
CONTRACT_TIME = (((1,), (1,)), ((), ()))

def exact_parts(values):
    high = lax.optimization_barrier(values.astype(jnp.bfloat16))
    remainder = values - high.astype(jnp.float32)
    middle = lax.optimization_barrier(remainder.astype(jnp.bfloat16))
    lowest = (remainder - middle.astype(jnp.float32)).astype(jnp.bfloat16)
    return jnp.concatenate([high, middle, lowest], axis=1)

def project_rows(values, rows):
    width = values.shape[1]
    product = lax.dot_general(exact_parts(values).astype(jnp.float32), rows.astype(jnp.float32), CONTRACT_ROWS, preferred_element_type=jnp.float32)
    return product[:width] + product[width:2 * width] + product[2 * width:]

def orthonormal(block):
    gram = jnp.dot(block.T, block, precision=HIGH)
    lower = jnp.linalg.cholesky(gram)
    inverse_t = jax.scipy.linalg.solve_triangular(lower, jnp.eye(gram.shape[0], dtype=jnp.float32), lower=True).T
    return jnp.dot(block, inverse_t, precision=HIGH)

def reference(anomaly, depth, cell_weight, test_matrix):
    levels = jnp.arange(anomaly.shape[2], dtype=jnp.int32)
    wet = (levels[None, None, :] < depth[:, :, None]).astype(jnp.float32)
    count = jnp.sum(wet)
    data = (anomaly.astype(jnp.float32) * jnp.sqrt(cell_weight)[:, :, None, None] * wet[..., None]).astype(jnp.bfloat16)
    rows = data.reshape(-1, anomaly.shape[3])
    sketch = jnp.dot(rows.astype(jnp.float32), test_matrix.astype(jnp.float32), preferred_element_type=jnp.float32)
    basis0 = orthonormal(sketch)
    timerank = project_rows(basis0, rows).astype(jnp.bfloat16)
    power = lax.dot_general(rows.astype(jnp.float32), timerank.astype(jnp.float32), CONTRACT_TIME, preferred_element_type=jnp.float32)
    basis = orthonormal(power)
    root = jnp.sqrt(count)
    eof = (basis * root).reshape(anomaly.shape[0], anomaly.shape[1], anomaly.shape[2], -1)
    coefficients = project_rows(basis, rows) / root
    return (eof, coefficients)
```

```python
import functools

import jax
import jax.numpy as jnp
from jax import lax
from jax.experimental import pallas as pl
from jax.experimental.pallas import tpu as pltpu
from jax.sharding import PartitionSpec as P

MESH = pl.DeviceIdType.MESH
F32 = jnp.float32
BF16 = jnp.bfloat16
OWNERS = 16
LAST = (((1,), (1,)), ((), ()))


def exact_parts(values):
    high = values.astype(BF16)
    remainder = values - high.astype(F32)
    middle = remainder.astype(BF16)
    lowest = (remainder - middle.astype(F32)).astype(BF16)
    return jnp.concatenate([high, middle, lowest], axis=0)


def sum_parts(stacked, width):
    return stacked[:width] + stacked[width : 2 * width] + stacked[2 * width :]


def dot_last(left, right):
    return lax.dot_general(left, right, LAST, preferred_element_type=F32)


def forward_eliminate(gram, sides, outs):
    rank = gram.shape[0]
    groups = rank // 8
    cols = []
    for g in range(groups):
        cols.append([jnp.broadcast_to(gram[8 * g :, c : c + 1], (rank - 8 * g, 128)) for c in range(8 * g, 8 * g + 8)])
    sides = [list(jnp.split(side, groups, axis=0)) for side in sides]
    rows = lax.broadcasted_iota(jnp.int32, (8, 128), 0)
    for k in range(rank):
        g, at = divmod(k, 8)
        column = cols[g][at]
        pivot = jnp.broadcast_to(column[at : at + 1, :], (8, 128))
        scale = lax.rsqrt(pivot)
        scale = scale * (1.5 - 0.5 * pivot * scale * scale)
        lower = []
        for i in range(g, groups):
            piece = column[8 * (i - g) : 8 * (i - g) + 8] * scale
            if i == g:
                piece = jnp.where(rows > at, piece, 0.0)
            lower.append(piece)
        for side, out in zip(sides, outs):
            width = side[0].shape[1]
            row = side[g][at : at + 1, :] * jnp.concatenate([scale[:1]] * (width // 128), axis=1)
            out[k : k + 1, :] = row
            for i in range(g, groups):
                side[i] = side[i] - jnp.concatenate([lower[i - g]] * (width // 128), axis=1) * row
        for i in range(g, groups):
            tall = lower[i - g] if i == groups - 1 else jnp.concatenate(lower[i - g :], axis=0)
            for c in range(8):
                if 8 * i + c > k:
                    cols[i][c] = cols[i][c] - tall * lower[i - g][c : c + 1, :]


def kernel(space_n, lev_n, rk_n, x_hbm, depth_ref, weight_ref, t_ref, eof_ref, coef_ref,
           x_buf, xf, data, t_all, mine, parts_a, sum_a, all_a, parts_b, sum_b, all_b,
           full, solved, solved_t, in_sem, t_sem, send_sem, recv_sem):
    n = space_n * lev_n * rk_n
    blocks, block_rows, time = x_hbm.shape
    cols = depth_ref.shape[1]
    levels = block_rows // cols
    half = t_ref.shape[0]
    rank = rk_n * half
    own_blocks = blocks // rk_n
    space, lev, rk = lax.axis_index("space"), lax.axis_index("lev"), lax.axis_index("rk")
    me = (space * lev_n + lev) * rk_n + rk

    def device(index):
        return {"space": index // (lev_n * rk_n), "lev": (index // rk_n) % lev_n, "rk": index % rk_n}

    def other(step):
        return (me + step) % n

    def each_other(body):
        if n <= 16:
            for step in range(1, n):
                body(step)
        else:
            @pl.loop(1, n)
            def _(step):
                body(step)

    def block_of(slot):
        return (rk * own_blocks + slot) % blocks

    def load(slot):
        return pltpu.make_async_copy(x_hbm.at[block_of(slot)], x_buf.at[slot], in_sem.at[slot])

    for slot in range(blocks):
        load(slot).start()

    barrier = pltpu.get_barrier_semaphore()
    each_other(lambda step: pl.semaphore_signal(barrier, inc=1, device_id=device(other(step)), device_id_type=MESH))

    t_all[rk] = t_ref[...]
    level0 = (lev * levels).astype(F32)

    def scale_slot(slot):
        block = block_of(slot)
        load(slot).wait()
        root = jnp.broadcast_to(jnp.sqrt(weight_ref[pl.ds(block, 1), :]), (128, cols)).T
        deep = jnp.broadcast_to(depth_ref[pl.ds(block, 1), :].astype(F32), (128, cols)).T
        for h in range(time // 128):
            xf[h] = x_buf[slot, :, 128 * h : 128 * h + 128].astype(F32)
        for l in range(levels):
            factor = jnp.where(level0 + l < deep, root, 0.0)
            for h in range(time // 128):
                value = xf[h, pl.ds(l, cols, stride=levels), :] * factor
                data[slot, l * cols : (l + 1) * cols, 128 * h : 128 * h + 128] = value.astype(BF16)

    def project(left, slot):
        rows = data[slot]
        parts = exact_parts(dot_last(left, rows))
        return sum_parts(jnp.dot(parts, rows, preferred_element_type=F32), rank)

    def pieces_of(full_value, extra):
        for p in range(OWNERS):
            q, h = divmod(p, 2)
            mine[p, 0:4, :] = full_value[4 * q : 4 * q + 4, 128 * h : 128 * h + 128]
            mine[p, 4:5, :] = extra

    def all_sum(value, extra, parts, total, gathered, base, between):
        pieces_of(value, extra)
        owner = None if n == OWNERS else me < OWNERS

        def when_owner(body):
            body() if owner is None else pl.when(owner)(body)

        def scatter(step):
            target = other(step)
            return pltpu.make_async_remote_copy(
                src_ref=mine.at[target % OWNERS], dst_ref=parts.at[me],
                send_sem=send_sem.at[base, target], recv_sem=recv_sem.at[base, me],
                device_id=device(target), device_id_type=MESH)

        def scattered(step):
            source = other(step)
            return pltpu.make_async_remote_copy(
                src_ref=mine.at[0], dst_ref=parts.at[source],
                send_sem=send_sem.at[base, source], recv_sem=recv_sem.at[base, source],
                device_id=device(source), device_id_type=MESH)

        def to_owner(step, body):
            body() if owner is None else pl.when(other(step) < OWNERS)(body)

        each_other(lambda step: to_owner(step, lambda: scatter(step).start()))
        between()

        def reduce():
            parts[me] = mine[me % OWNERS]
            each_other(lambda step: scattered(step).wait_recv())
            total[...] = jnp.sum(parts[...], axis=0)
            gathered[me % OWNERS] = total[...]

        when_owner(reduce)

        def spread(step):
            target = other(step)
            return pltpu.make_async_remote_copy(
                src_ref=total, dst_ref=gathered.at[me % OWNERS],
                send_sem=send_sem.at[base + 1, target], recv_sem=recv_sem.at[base + 1, me],
                device_id=device(target), device_id_type=MESH)

        def spreaded(step):
            source = other(step)
            return pltpu.make_async_remote_copy(
                src_ref=total, dst_ref=gathered.at[source % OWNERS],
                send_sem=send_sem.at[base + 1, source], recv_sem=recv_sem.at[base + 1, source],
                device_id=device(source), device_id_type=MESH)

        when_owner(lambda: each_other(lambda step: spread(step).start()))
        each_other(lambda step: to_owner(step, lambda: scatter(step).wait_send()))
        each_other(lambda step: to_owner(step, lambda: spreaded(step).wait_recv()))
        for p in range(OWNERS):
            q, h = divmod(p, 2)
            full[4 * q : 4 * q + 4, 128 * h : 128 * h + 128] = gathered[p, 0:4, :]

        def finish():
            when_owner(lambda: each_other(lambda step: spread(step).wait_send()))

        return full[...], gathered[0, 4:5, :], finish

    def scale_first(slot, carry):
        scale_slot(slot)
        return carry

    lax.fori_loop(0, own_blocks, scale_first, 0)

    pl.semaphore_wait(barrier, n - 1)
    partner = {"rk": 1 - rk}
    t_copy = pltpu.make_async_remote_copy(
        src_ref=t_ref, dst_ref=t_all.at[rk], send_sem=t_sem.at[0], recv_sem=t_sem.at[1],
        device_id=partner, device_id_type=MESH)
    t_copy.start()
    t_copy.wait()
    test = t_all[...].reshape(rank, time)

    depths = depth_ref[pl.ds(rk * own_blocks, own_blocks), :].astype(F32)
    wet = jnp.clip(depths - level0, 0.0, float(levels))
    local_count = jnp.broadcast_to(jnp.sum(wet, keepdims=True), (1, 128))

    def both(left):
        return lax.fori_loop(0, own_blocks, lambda slot, acc: acc + project(left, slot), jnp.zeros((rank, time), F32))

    first = both(test)

    def rest():
        lax.fori_loop(own_blocks, blocks, scale_first, 0)

    z, count, finish_a = all_sum(first, local_count, parts_a, sum_a, all_a, 0, rest)
    gram0 = sum_parts(dot_last(exact_parts(z), test), rank)
    forward_eliminate(gram0, [z], [solved])
    finish_a()
    timerank = solved[...].astype(BF16)

    second = both(timerank)
    w, _, finish_b = all_sum(second, local_count, parts_b, sum_b, all_b, 2, lambda: None)
    gram1 = sum_parts(dot_last(exact_parts(w), timerank), rank)
    forward_eliminate(gram1, [w, timerank.astype(F32)], [solved, solved_t])
    finish_b()
    root_count = jnp.sqrt(jnp.concatenate([count] * (time // 128), axis=1))
    own = pl.ds(pl.multiple_of(rk * half, half), half)
    coef_ref[...] = solved[own, :] / root_count
    pattern = exact_parts(solved_t[own, :] * root_count)

    def emit(slot, carry):
        e = sum_parts(dot_last(pattern, data[slot]), half)
        block = block_of(slot)
        for l in range(levels):
            eof_ref[block, l] = e[:, l * cols : (l + 1) * cols]
        return carry

    lax.fori_loop(0, blocks, emit, 0)


def local(space_n, lev_n, rk_n, anomaly, depth, cell_weight, test_matrix):
    blocks, cols, levels, time = anomaly.shape
    half = test_matrix.shape[1]
    rank = rk_n * half
    n = space_n * lev_n * rk_n
    piece = (5, 128)
    vmem = pl.BlockSpec(memory_space=pltpu.VMEM)
    eof, coefficients = pl.pallas_call(
        functools.partial(kernel, space_n, lev_n, rk_n),
        out_shape=(jax.ShapeDtypeStruct((blocks, levels, half, cols), F32), jax.ShapeDtypeStruct((half, time), F32)),
        in_specs=[pl.BlockSpec(memory_space=pl.ANY), vmem, vmem, vmem],
        out_specs=(vmem, vmem),
        scratch_shapes=[
            pltpu.VMEM((blocks, cols * levels, time), BF16),
            pltpu.VMEM((time // 128, cols * levels, 128), F32),
            pltpu.VMEM((blocks, cols * levels, time), BF16),
            pltpu.VMEM((rk_n, half, time), BF16),
            pltpu.VMEM((OWNERS, *piece), F32),
            pltpu.VMEM((n, *piece), F32), pltpu.VMEM(piece, F32), pltpu.VMEM((OWNERS, *piece), F32),
            pltpu.VMEM((n, *piece), F32), pltpu.VMEM(piece, F32), pltpu.VMEM((OWNERS, *piece), F32),
            pltpu.VMEM((rank, time), F32), pltpu.VMEM((rank, time), F32), pltpu.VMEM((rank, time), F32),
            pltpu.SemaphoreType.DMA((blocks,)),
            pltpu.SemaphoreType.DMA((2,)),
            pltpu.SemaphoreType.DMA((4, n)),
            pltpu.SemaphoreType.DMA((4, n)),
        ],
        compiler_params=pltpu.CompilerParams(
            collective_id=0, has_side_effects=True, vmem_limit_bytes=40 * 1024 * 1024),
        name="eof_power_pass",
    )(anomaly.reshape(blocks, cols * levels, time), depth, cell_weight, test_matrix.T)
    return eof.transpose(0, 3, 1, 2), coefficients


def solution(mesh):
    placed = (
        P(("grp", "space"), None, "lev", None),
        P(("grp", "space"), None),
        P(("grp", "space"), None),
        P(None, "rk"),
    )
    sizes = [mesh.shape[axis] for axis in ("space", "lev", "rk")]
    return jax.shard_map(
        functools.partial(local, *sizes),
        mesh=mesh,
        in_specs=placed,
        out_specs=(P(("grp", "space"), None, "lev", "rk"), P(("grp", "rk"), None)),
        check_vma=False,
    )
```

```python
import functools

import jax
import jax.numpy as jnp
from jax import lax
from jax.experimental import pallas as pl
from jax.experimental.pallas import tpu as pltpu
from jax.sharding import PartitionSpec as P

MESH = pl.DeviceIdType.MESH
F32 = jnp.float32
BF16 = jnp.bfloat16
OWNERS = 8
LAST = (((1,), (1,)), ((), ()))


def exact_parts(values):
    high = values.astype(BF16)
    remainder = values - high.astype(F32)
    middle = remainder.astype(BF16)
    lowest = (remainder - middle.astype(F32)).astype(BF16)
    return jnp.concatenate([high, middle, lowest], axis=0)


def sum_parts(stacked, width):
    return stacked[:width] + stacked[width : 2 * width] + stacked[2 * width :]


def dot_last(left, right):
    return lax.dot_general(left, right, LAST, preferred_element_type=F32)


def forward_eliminate(gram, sides, outs):
    rank = gram.shape[0]
    groups = rank // 8
    cols = []
    for g in range(groups):
        cols.append([jnp.broadcast_to(gram[8 * g :, c : c + 1], (rank - 8 * g, 128)) for c in range(8 * g, 8 * g + 8)])
    sides = [list(jnp.split(side, groups, axis=0)) for side in sides]
    rows = lax.broadcasted_iota(jnp.int32, (8, 128), 0)
    for k in range(rank):
        g, at = divmod(k, 8)
        column = cols[g][at]
        pivot = jnp.broadcast_to(column[at : at + 1, :], (8, 128))
        scale = lax.rsqrt(pivot)
        scale = scale * (1.5 - 0.5 * pivot * scale * scale)
        lower = []
        for i in range(g, groups):
            piece = column[8 * (i - g) : 8 * (i - g) + 8] * scale
            if i == g:
                piece = jnp.where(rows > at, piece, 0.0)
            lower.append(piece)
        for side, out in zip(sides, outs):
            width = side[0].shape[1]
            row = side[g][at : at + 1, :] * jnp.concatenate([scale[:1]] * (width // 128), axis=1)
            out[k : k + 1, :] = row
            for i in range(g, groups):
                side[i] = side[i] - jnp.concatenate([lower[i - g]] * (width // 128), axis=1) * row
        for i in range(g, groups):
            tall = lower[i - g] if i == groups - 1 else jnp.concatenate(lower[i - g :], axis=0)
            for c in range(8):
                if 8 * i + c > k:
                    cols[i][c] = cols[i][c] - tall * lower[i - g][c : c + 1, :]


def kernel(space_n, lev_n, rk_n, x_hbm, depth_hbm, weight_hbm, t_hbm, eof_ref, coef_ref,
           depth_ref, weight_ref, t_ref, x_buf, xf, data, t_all, mine, parts, all_g, g_parts,
           solved, solved_t, small_sem, in_sem, core_sem, send_sem, recv_sem):
    chips = space_n * lev_n
    blocks, block_rows, time = x_hbm.shape
    cols = depth_ref.shape[1]
    levels = block_rows // cols
    half = t_ref.shape[0]
    rank = rk_n * half
    g_half = time // rk_n
    piece = g_half // OWNERS
    space, lev, rk = lax.axis_index("space"), lax.axis_index("lev"), lax.axis_index("rk")
    me = space * lev_n + lev
    partner = {"rk": 1 - rk}

    def device(chip):
        return {"space": chip // lev_n, "lev": chip % lev_n}

    def each_other(body):
        if chips <= 16:
            for step in range(1, chips):
                body((me + step) % chips)
        else:
            @pl.loop(1, chips)
            def _(step):
                body((me + step) % chips)

    def if_owner(chip, body):
        body() if chips == OWNERS else pl.when(chip < OWNERS)(body)

    def load(slot):
        return pltpu.make_async_copy(x_hbm.at[slot], x_buf.at[slot], in_sem.at[slot])

    smalls = [
        pltpu.make_async_copy(source, target, small_sem.at[i])
        for i, (source, target) in enumerate(((t_hbm, t_ref), (weight_hbm, weight_ref), (depth_hbm, depth_ref)))
    ]
    for small in smalls:
        small.start()
    for slot in range(blocks):
        load(slot).start()

    barrier = pltpu.get_barrier_semaphore()
    pl.semaphore_signal(barrier, inc=1, device_id=partner, device_id_type=MESH)
    each_other(lambda chip: pl.semaphore_signal(barrier, inc=1, device_id=device(chip), device_id_type=MESH))

    for small in smalls:
        small.wait()
    t_all[rk] = t_ref[...]
    level0 = (lev * levels).astype(F32)

    def scale_slot(slot):
        load(slot).wait()
        root = jnp.broadcast_to(jnp.sqrt(weight_ref[pl.ds(slot, 1), :]), (128, cols)).T
        deep = jnp.broadcast_to(depth_ref[pl.ds(slot, 1), :].astype(F32), (128, cols)).T
        for h in range(time // 128):
            xf[h] = x_buf[slot, :, 128 * h : 128 * h + 128].astype(F32)
        for l in range(levels):
            factor = jnp.where(level0 + l < deep, root, 0.0)
            for h in range(time // 128):
                value = xf[h, pl.ds(l, cols, stride=levels), :] * factor
                data[slot, l * cols : (l + 1) * cols, 128 * h : 128 * h + 128] = value.astype(BF16)

    g_own = pl.ds(pl.multiple_of(rk * g_half, g_half), g_half)

    def gram_slot(slot, total):
        scale_slot(slot)
        return total + lax.dot_general(
            data[slot, :, g_own], data[slot], (((0,), (0,)), ((), ())), preferred_element_type=F32)

    gram = lax.fori_loop(0, blocks, gram_slot, jnp.zeros((g_half, time), F32))
    wet = jnp.clip(depth_ref[...].astype(F32) - level0, 0.0, float(levels))
    local_count = jnp.broadcast_to(jnp.sum(wet, keepdims=True), (1, time))
    for p in range(OWNERS):
        mine[p, 0:piece, :] = gram[piece * p : piece * (p + 1)]
        mine[p, piece : piece + 1, :] = local_count

    pl.semaphore_wait(barrier, chips)

    def scatter(target):
        return pltpu.make_async_remote_copy(
            src_ref=mine.at[target % OWNERS], dst_ref=parts.at[me],
            send_sem=send_sem.at[0, target], recv_sem=recv_sem.at[0, me],
            device_id=device(target), device_id_type=MESH)

    def scattered(source):
        return pltpu.make_async_remote_copy(
            src_ref=mine.at[0], dst_ref=parts.at[source],
            send_sem=send_sem.at[0, source], recv_sem=recv_sem.at[0, source],
            device_id=device(source), device_id_type=MESH)

    def spread(target):
        return pltpu.make_async_remote_copy(
            src_ref=all_g.at[rk, me % OWNERS], dst_ref=all_g.at[rk, me % OWNERS],
            send_sem=send_sem.at[1, target], recv_sem=recv_sem.at[1, me],
            device_id=device(target), device_id_type=MESH)

    def spreaded(source):
        return pltpu.make_async_remote_copy(
            src_ref=all_g.at[rk, source % OWNERS], dst_ref=all_g.at[rk, source % OWNERS],
            send_sem=send_sem.at[1, source], recv_sem=recv_sem.at[1, source],
            device_id=device(source), device_id_type=MESH)

    each_other(lambda chip: if_owner(chip, lambda: scatter(chip).start()))
    t_copy = pltpu.make_async_remote_copy(
        src_ref=t_ref, dst_ref=t_all.at[rk], send_sem=core_sem.at[0], recv_sem=core_sem.at[1],
        device_id=partner, device_id_type=MESH)
    t_copy.start()

    def reduce():
        parts[me] = mine[me % OWNERS]
        each_other(lambda chip: scattered(chip).wait_recv())
        all_g[rk, me % OWNERS] = jnp.sum(parts[...], axis=0)
        each_other(lambda chip: spread(chip).start())

    if_owner(me, reduce)
    t_copy.wait()
    each_other(lambda chip: if_owner(chip, lambda: scatter(chip).wait_send()))
    each_other(lambda chip: if_owner(chip, lambda: spreaded(chip).wait_recv()))
    swap = pltpu.make_async_remote_copy(
        src_ref=all_g.at[rk], dst_ref=all_g.at[rk], send_sem=core_sem.at[2], recv_sem=core_sem.at[3],
        device_id=partner, device_id_type=MESH)
    swap.start()
    if_owner(me, lambda: each_other(lambda chip: spread(chip).wait_send()))
    test = t_all[...].reshape(rank, time)
    swap.wait()

    whole = all_g[:, :, 0:piece, :].reshape(time, time)
    count = all_g[0, 0, piece : piece + 1, :]
    high = whole.astype(BF16)
    remainder = whole - high.astype(F32)
    middle = remainder.astype(BF16)
    g_parts[0] = high
    g_parts[1] = middle
    g_parts[2] = (remainder - middle.astype(F32)).astype(BF16)

    def times_g(left):
        products = [jnp.dot(left, g_parts[i], preferred_element_type=F32) for i in range(3)]
        return products[0] + (products[1] + products[2])

    z = times_g(test)
    gram0 = sum_parts(dot_last(exact_parts(z), test), rank)
    forward_eliminate(gram0, [z], [solved])
    timerank = solved[...].astype(BF16)

    w = times_g(timerank)
    gram1 = sum_parts(dot_last(exact_parts(w), timerank), rank)
    forward_eliminate(gram1, [w, timerank.astype(F32)], [solved, solved_t])
    root_count = jnp.sqrt(count)
    own = pl.ds(pl.multiple_of(rk * half, half), half)
    coef_ref[...] = solved[own, :] / root_count
    pattern = exact_parts(solved_t[own, :] * root_count)

    def emit(slot, carry):
        e = sum_parts(dot_last(pattern, data[slot]), half)
        for l in range(levels):
            eof_ref[slot, l] = e[:, l * cols : (l + 1) * cols]
        return carry

    lax.fori_loop(0, blocks, emit, 0)


def local(space_n, lev_n, rk_n, anomaly, depth, cell_weight, test_matrix):
    blocks, cols, levels, time = anomaly.shape
    half = test_matrix.shape[1]
    rank = rk_n * half
    chips = space_n * lev_n
    piece = (time // (rk_n * OWNERS) + 1, time)
    vmem = pl.BlockSpec(memory_space=pltpu.VMEM)
    eof, coefficients = pl.pallas_call(
        functools.partial(kernel, space_n, lev_n, rk_n),
        out_shape=(jax.ShapeDtypeStruct((blocks, levels, half, cols), F32), jax.ShapeDtypeStruct((half, time), F32)),
        in_specs=[pl.BlockSpec(memory_space=pltpu.HBM)] * 4,
        out_specs=(vmem, vmem),
        scratch_shapes=[
            pltpu.VMEM((blocks, cols), depth.dtype),
            pltpu.VMEM((blocks, cols), F32),
            pltpu.VMEM((half, time), BF16),
            pltpu.VMEM((blocks, cols * levels, time), BF16),
            pltpu.VMEM((time // 128, cols * levels, 128), F32),
            pltpu.VMEM((blocks, cols * levels, time), BF16),
            pltpu.VMEM((rk_n, half, time), BF16),
            pltpu.VMEM((OWNERS, *piece), F32),
            pltpu.VMEM((chips, *piece), F32),
            pltpu.VMEM((rk_n, OWNERS, *piece), F32),
            pltpu.VMEM((3, time, time), BF16),
            pltpu.VMEM((rank, time), F32),
            pltpu.VMEM((rank, time), F32),
            pltpu.SemaphoreType.DMA((3,)),
            pltpu.SemaphoreType.DMA((blocks,)),
            pltpu.SemaphoreType.DMA((4,)),
            pltpu.SemaphoreType.DMA((2, chips)),
            pltpu.SemaphoreType.DMA((2, chips)),
        ],
        compiler_params=pltpu.CompilerParams(
            collective_id=0, has_side_effects=True, vmem_limit_bytes=60 * 1024 * 1024),
        name="eof_power_pass",
    )(anomaly.reshape(blocks, cols * levels, time), depth, cell_weight, test_matrix.T)
    return eof.transpose(0, 3, 1, 2), coefficients


def solution(mesh):
    placed = (
        P(("grp", "space"), None, "lev", None),
        P(("grp", "space"), None),
        P(("grp", "space"), None),
        P(None, "rk"),
    )
    sizes = [mesh.shape[axis] for axis in ("space", "lev", "rk")]
    return jax.shard_map(
        functools.partial(local, *sizes),
        mesh=mesh,
        in_specs=placed,
        out_specs=(P(("grp", "space"), None, "lev", "rk"), P(("grp", "rk"), None)),
        check_vma=False,
    )
```

```python
import functools

import jax
import jax.numpy as jnp
from jax import lax
from jax.experimental import pallas as pl
from jax.experimental.pallas import tpu as pltpu
from jax.sharding import PartitionSpec as P

MESH = pl.DeviceIdType.MESH
F32 = jnp.float32
BF16 = jnp.bfloat16
OWNERS = 8
LAST = (((1,), (1,)), ((), ()))


def exact_parts(values):
    high = values.astype(BF16)
    remainder = values - high.astype(F32)
    middle = remainder.astype(BF16)
    lowest = (remainder - middle.astype(F32)).astype(BF16)
    return jnp.concatenate([high, middle, lowest], axis=0)


def sum_parts(stacked, width):
    return stacked[:width] + stacked[width : 2 * width] + stacked[2 * width :]


def dot_last(left, right):
    return lax.dot_general(left, right, LAST, preferred_element_type=F32)


def forward_eliminate(gram, sides, outs):
    rank = gram.shape[0]
    groups = rank // 8
    cols = []
    for g in range(groups):
        cols.append([jnp.broadcast_to(gram[8 * g :, c : c + 1], (rank - 8 * g, 128)) for c in range(8 * g, 8 * g + 8)])
    sides = [list(jnp.split(side, groups, axis=0)) for side in sides]
    rows = lax.broadcasted_iota(jnp.int32, (8, 128), 0)
    for k in range(rank):
        g, at = divmod(k, 8)
        column = cols[g][at]
        pivot = jnp.broadcast_to(column[at : at + 1, :], (8, 128))
        scale = lax.rsqrt(pivot)
        scale = scale * (1.5 - 0.5 * pivot * scale * scale)
        lower = []
        for i in range(g, groups):
            piece = column[8 * (i - g) : 8 * (i - g) + 8] * scale
            if i == g:
                piece = jnp.where(rows > at, piece, 0.0)
            lower.append(piece)
        for side, out in zip(sides, outs):
            width = side[0].shape[1]
            row = side[g][at : at + 1, :] * jnp.concatenate([scale[:1]] * (width // 128), axis=1)
            out[k : k + 1, :] = row
            for i in range(g, groups):
                side[i] = side[i] - jnp.concatenate([lower[i - g]] * (width // 128), axis=1) * row
        for i in range(g, groups):
            tall = lower[i - g] if i == groups - 1 else jnp.concatenate(lower[i - g :], axis=0)
            for c in range(8):
                if 8 * i + c > k:
                    cols[i][c] = cols[i][c] - tall * lower[i - g][c : c + 1, :]


def kernel(space_n, lev_n, rk_n, x_hbm, depth_hbm, weight_hbm, t_hbm, eof_ref, coef_ref,
           depth_ref, weight_ref, t_ref, x_buf, xf, data, t_all, g_local, g_peer, mine, parts, all_g, g_parts,
           solved, solved_t, small_sem, in_sem, core_sem, send_sem, recv_sem):
    chips = space_n * lev_n
    blocks, block_rows, time = x_hbm.shape
    cols = depth_ref.shape[1]
    levels = block_rows // cols
    half = t_ref.shape[0]
    rank = rk_n * half
    g_half = time // rk_n
    piece = g_half // OWNERS
    space, lev, rk = lax.axis_index("space"), lax.axis_index("lev"), lax.axis_index("rk")
    me = space * lev_n + lev
    partner = {"rk": 1 - rk}

    def device(chip):
        return {"space": chip // lev_n, "lev": chip % lev_n}

    def each_other(body):
        if chips <= 16:
            for step in range(1, chips):
                body((me + step) % chips)
        else:
            @pl.loop(1, chips)
            def _(step):
                body((me + step) % chips)

    def if_owner(chip, body):
        body() if chips == OWNERS else pl.when(chip < OWNERS)(body)

    own_blocks = blocks // rk_n

    def block_of(slot):
        return (rk * own_blocks + slot) % blocks

    def load(slot):
        return pltpu.make_async_copy(x_hbm.at[block_of(slot)], x_buf.at[slot], in_sem.at[slot])

    smalls = [
        pltpu.make_async_copy(source, target, small_sem.at[i])
        for i, (source, target) in enumerate(((t_hbm, t_ref), (weight_hbm, weight_ref), (depth_hbm, depth_ref)))
    ]
    for small in smalls:
        small.start()
    for slot in range(blocks):
        load(slot).start()

    barrier = pltpu.get_barrier_semaphore()
    pl.semaphore_signal(barrier, inc=1, device_id=partner, device_id_type=MESH)
    each_other(lambda chip: pl.semaphore_signal(barrier, inc=1, device_id=device(chip), device_id_type=MESH))

    for small in smalls:
        small.wait()
    t_all[rk] = t_ref[...]
    level0 = (lev * levels).astype(F32)

    def scale_slot(slot):
        block = block_of(slot)
        load(slot).wait()
        root = jnp.broadcast_to(jnp.sqrt(weight_ref[pl.ds(block, 1), :]), (128, cols)).T
        deep = jnp.broadcast_to(depth_ref[pl.ds(block, 1), :].astype(F32), (128, cols)).T
        for h in range(time // 128):
            xf[h] = x_buf[slot, :, 128 * h : 128 * h + 128].astype(F32)
        for l in range(levels):
            factor = jnp.where(level0 + l < deep, root, 0.0)
            for h in range(time // 128):
                value = xf[h, pl.ds(l, cols, stride=levels), :] * factor
                data[slot, l * cols : (l + 1) * cols, 128 * h : 128 * h + 128] = value.astype(BF16)

    def gram_slot(slot, total):
        scale_slot(slot)
        return total + lax.dot_general(
            data[slot], data[slot], (((0,), (0,)), ((), ())), preferred_element_type=F32)

    gram = lax.fori_loop(0, own_blocks, gram_slot, jnp.zeros((time, time), F32))
    for r in range(rk_n):
        g_local[r] = gram[g_half * r : g_half * (r + 1)]
    wet = jnp.clip(depth_ref[...].astype(F32) - level0, 0.0, float(levels))
    local_count = jnp.broadcast_to(jnp.sum(wet, keepdims=True), (1, time))

    pl.semaphore_wait(barrier, chips)
    halves = pltpu.make_async_remote_copy(
        src_ref=g_local.at[1 - rk], dst_ref=g_peer, send_sem=core_sem.at[4], recv_sem=core_sem.at[5],
        device_id=partner, device_id_type=MESH)
    halves.start()
    t_copy = pltpu.make_async_remote_copy(
        src_ref=t_ref, dst_ref=t_all.at[rk], send_sem=core_sem.at[0], recv_sem=core_sem.at[1],
        device_id=partner, device_id_type=MESH)
    t_copy.start()
    halves.wait()
    for p in range(OWNERS):
        rows = slice(piece * p, piece * (p + 1))
        mine[p, 0:piece, :] = g_local[rk, rows, :] + g_peer[rows, :]
        mine[p, piece : piece + 1, :] = local_count

    def scatter(target):
        return pltpu.make_async_remote_copy(
            src_ref=mine.at[target % OWNERS], dst_ref=parts.at[me],
            send_sem=send_sem.at[0, target], recv_sem=recv_sem.at[0, me],
            device_id=device(target), device_id_type=MESH)

    def scattered(source):
        return pltpu.make_async_remote_copy(
            src_ref=mine.at[0], dst_ref=parts.at[source],
            send_sem=send_sem.at[0, source], recv_sem=recv_sem.at[0, source],
            device_id=device(source), device_id_type=MESH)

    def spread(target):
        return pltpu.make_async_remote_copy(
            src_ref=all_g.at[rk, me % OWNERS], dst_ref=all_g.at[rk, me % OWNERS],
            send_sem=send_sem.at[1, target], recv_sem=recv_sem.at[1, me],
            device_id=device(target), device_id_type=MESH)

    def spreaded(source):
        return pltpu.make_async_remote_copy(
            src_ref=all_g.at[rk, source % OWNERS], dst_ref=all_g.at[rk, source % OWNERS],
            send_sem=send_sem.at[1, source], recv_sem=recv_sem.at[1, source],
            device_id=device(source), device_id_type=MESH)

    each_other(lambda chip: if_owner(chip, lambda: scatter(chip).start()))
    def scale_rest(slot, carry):
        scale_slot(slot)
        return carry

    lax.fori_loop(own_blocks, blocks, scale_rest, 0)

    def reduce():
        parts[me] = mine[me % OWNERS]
        each_other(lambda chip: scattered(chip).wait_recv())
        all_g[rk, me % OWNERS] = jnp.sum(parts[...], axis=0)
        each_other(lambda chip: spread(chip).start())

    if_owner(me, reduce)
    t_copy.wait()
    each_other(lambda chip: if_owner(chip, lambda: scatter(chip).wait_send()))
    each_other(lambda chip: if_owner(chip, lambda: spreaded(chip).wait_recv()))
    swap = pltpu.make_async_remote_copy(
        src_ref=all_g.at[rk], dst_ref=all_g.at[rk], send_sem=core_sem.at[2], recv_sem=core_sem.at[3],
        device_id=partner, device_id_type=MESH)
    swap.start()
    if_owner(me, lambda: each_other(lambda chip: spread(chip).wait_send()))
    test = t_all[...].reshape(rank, time)
    swap.wait()

    whole = all_g[:, :, 0:piece, :].reshape(time, time)
    count = all_g[0, 0, piece : piece + 1, :]
    high = whole.astype(BF16)
    remainder = whole - high.astype(F32)
    middle = remainder.astype(BF16)
    g_parts[0] = high
    g_parts[1] = middle
    g_parts[2] = (remainder - middle.astype(F32)).astype(BF16)

    def times_g(left):
        products = [jnp.dot(left, g_parts[i], preferred_element_type=F32) for i in range(3)]
        return products[0] + (products[1] + products[2])

    z = times_g(test)
    gram0 = sum_parts(dot_last(exact_parts(z), test), rank)
    forward_eliminate(gram0, [z], [solved])
    timerank = solved[...].astype(BF16)

    w = times_g(timerank)
    gram1 = sum_parts(dot_last(exact_parts(w), timerank), rank)
    forward_eliminate(gram1, [w, timerank.astype(F32)], [solved, solved_t])
    root_count = jnp.sqrt(count)
    own = pl.ds(pl.multiple_of(rk * half, half), half)
    coef_ref[...] = solved[own, :] / root_count
    pattern = exact_parts(solved_t[own, :] * root_count)

    def emit(slot, carry):
        e = sum_parts(dot_last(pattern, data[slot]), half)
        block = block_of(slot)
        for l in range(levels):
            eof_ref[block, l] = e[:, l * cols : (l + 1) * cols]
        return carry

    lax.fori_loop(0, blocks, emit, 0)


def local(space_n, lev_n, rk_n, anomaly, depth, cell_weight, test_matrix):
    blocks, cols, levels, time = anomaly.shape
    half = test_matrix.shape[1]
    rank = rk_n * half
    chips = space_n * lev_n
    piece = (time // (rk_n * OWNERS) + 1, time)
    vmem = pl.BlockSpec(memory_space=pltpu.VMEM)
    eof, coefficients = pl.pallas_call(
        functools.partial(kernel, space_n, lev_n, rk_n),
        out_shape=(pltpu.VMEM((blocks, levels, half, cols), F32), pltpu.VMEM((half, time), F32)),
        in_specs=[pl.BlockSpec(memory_space=pltpu.HBM)] * 4,
        out_specs=(vmem, vmem),
        scratch_shapes=[
            pltpu.VMEM((blocks, cols), depth.dtype),
            pltpu.VMEM((blocks, cols), F32),
            pltpu.VMEM((half, time), BF16),
            pltpu.VMEM((blocks, cols * levels, time), BF16),
            pltpu.VMEM((time // 128, cols * levels, 128), F32),
            pltpu.VMEM((blocks, cols * levels, time), BF16),
            pltpu.VMEM((rk_n, half, time), BF16),
            pltpu.VMEM((rk_n, time // rk_n, time), F32),
            pltpu.VMEM((time // rk_n, time), F32),
            pltpu.VMEM((OWNERS, *piece), F32),
            pltpu.VMEM((chips, *piece), F32),
            pltpu.VMEM((rk_n, OWNERS, *piece), F32),
            pltpu.VMEM((3, time, time), BF16),
            pltpu.VMEM((rank, time), F32),
            pltpu.VMEM((rank, time), F32),
            pltpu.SemaphoreType.DMA((3,)),
            pltpu.SemaphoreType.DMA((blocks,)),
            pltpu.SemaphoreType.DMA((6,)),
            pltpu.SemaphoreType.DMA((2, chips)),
            pltpu.SemaphoreType.DMA((2, chips)),
        ],
        compiler_params=pltpu.CompilerParams(
            collective_id=0, has_side_effects=True, vmem_limit_bytes=60 * 1024 * 1024),
        name="eof_power_pass",
    )(anomaly.reshape(blocks, cols * levels, time), depth, cell_weight, test_matrix.T)
    return eof.transpose(0, 3, 1, 2), coefficients


def solution(mesh):
    placed = (
        P(("grp", "space"), None, "lev", None),
        P(("grp", "space"), None),
        P(("grp", "space"), None),
        P(None, "rk"),
    )
    sizes = [mesh.shape[axis] for axis in ("space", "lev", "rk")]
    return jax.shard_map(
        functools.partial(local, *sizes),
        mesh=mesh,
        in_specs=placed,
        out_specs=(P(("grp", "space"), None, "lev", "rk"), P(("grp", "rk"), None)),
        check_vma=False,
    )
```

```python
import functools

import jax
import jax.numpy as jnp
from jax import lax
from jax.experimental import pallas as pl
from jax.experimental.pallas import tpu as pltpu
from jax.sharding import PartitionSpec as P

MESH = pl.DeviceIdType.MESH
F32 = jnp.float32
BF16 = jnp.bfloat16
OWNERS = 8
LAST = (((1,), (1,)), ((), ()))


def exact_parts(values):
    high = values.astype(BF16)
    remainder = values - high.astype(F32)
    middle = remainder.astype(BF16)
    lowest = (remainder - middle.astype(F32)).astype(BF16)
    return jnp.concatenate([high, middle, lowest], axis=0)


def sum_parts(stacked, width):
    return stacked[:width] + stacked[width : 2 * width] + stacked[2 * width :]


def dot_last(left, right):
    return lax.dot_general(left, right, LAST, preferred_element_type=F32)


def forward_eliminate(gram, sides, outs):
    rank = gram.shape[0]
    groups = rank // 8
    cols = []
    for g in range(groups):
        cols.append([jnp.broadcast_to(gram[8 * g :, c : c + 1], (rank - 8 * g, 128)) for c in range(8 * g, 8 * g + 8)])
    sides = [list(jnp.split(side, groups, axis=0)) for side in sides]
    rows = lax.broadcasted_iota(jnp.int32, (8, 128), 0)
    for k in range(rank):
        g, at = divmod(k, 8)
        column = cols[g][at]
        pivot = jnp.broadcast_to(column[at : at + 1, :], (8, 128))
        scale = lax.rsqrt(pivot)
        scale = scale * (1.5 - 0.5 * pivot * scale * scale)
        lower = []
        for i in range(g, groups):
            piece = column[8 * (i - g) : 8 * (i - g) + 8] * scale
            if i == g:
                piece = jnp.where(rows > at, piece, 0.0)
            lower.append(piece)
        for side, out in zip(sides, outs):
            width = side[0].shape[1]
            row = side[g][at : at + 1, :] * jnp.concatenate([scale[:1]] * (width // 128), axis=1)
            out[k : k + 1, :] = row
            for i in range(g, groups):
                side[i] = side[i] - jnp.concatenate([lower[i - g]] * (width // 128), axis=1) * row
        for i in range(g, groups):
            tall = lower[i - g] if i == groups - 1 else jnp.concatenate(lower[i - g :], axis=0)
            for c in range(8):
                if 8 * i + c > k:
                    cols[i][c] = cols[i][c] - tall * lower[i - g][c : c + 1, :]


def kernel(space_n, lev_n, rk_n, x_hbm, depth_hbm, weight_hbm, t_hbm, eof_ref, coef_ref,
           depth_ref, weight_ref, t_ref, x_buf, xf, data, t_all, g_local, g_peer, mine, parts, all_g, g_parts,
           solved, solved_t, small_sem, in_sem, core_sem, send_sem, recv_sem):
    chips = space_n * lev_n
    blocks, block_rows, time = x_hbm.shape
    cols = depth_ref.shape[1]
    levels = block_rows // cols
    half = t_ref.shape[0]
    rank = rk_n * half
    g_half = time // rk_n
    piece = g_half // OWNERS
    space, lev, rk = lax.axis_index("space"), lax.axis_index("lev"), lax.axis_index("rk")
    me = space * lev_n + lev
    partner = {"rk": 1 - rk}

    def device(chip):
        return {"space": chip // lev_n, "lev": chip % lev_n}

    def each_other(body):
        if chips <= 16:
            for step in range(1, chips):
                body((me + step) % chips)
        else:
            @pl.loop(1, chips)
            def _(step):
                body((me + step) % chips)

    def if_owner(chip, body):
        body() if chips == OWNERS else pl.when(chip < OWNERS)(body)

    own_blocks = blocks // rk_n

    def block_of(slot):
        return (rk * own_blocks + slot) % blocks

    def load(slot):
        return pltpu.make_async_copy(x_hbm.at[block_of(slot)], x_buf.at[slot], in_sem.at[slot])

    smalls = [
        pltpu.make_async_copy(source, target, small_sem.at[i])
        for i, (source, target) in enumerate(((t_hbm, t_ref), (weight_hbm, weight_ref), (depth_hbm, depth_ref)))
    ]
    load(0).start()
    for small in smalls:
        small.start()
    for slot in range(1, own_blocks):
        load(slot).start()

    barrier = pltpu.get_barrier_semaphore()
    pl.semaphore_signal(barrier, inc=1, device_id=partner, device_id_type=MESH)
    each_other(lambda chip: pl.semaphore_signal(barrier, inc=1, device_id=device(chip), device_id_type=MESH))

    for slot in range(own_blocks, blocks):
        load(slot).start()

    for small in smalls:
        small.wait()
    t_all[rk] = t_ref[...]
    level0 = (lev * levels).astype(F32)

    def scale_slot(slot):
        block = block_of(slot)
        load(slot).wait()
        root = jnp.broadcast_to(jnp.sqrt(weight_ref[pl.ds(block, 1), :]), (128, cols)).T
        deep = jnp.broadcast_to(depth_ref[pl.ds(block, 1), :].astype(F32), (128, cols)).T
        for h in range(time // 128):
            xf[slot % 2, h] = x_buf[slot, :, 128 * h : 128 * h + 128].astype(F32)
        for l in range(levels):
            factor = jnp.where(level0 + l < deep, root, 0.0)
            for h in range(time // 128):
                value = xf[slot % 2, h, pl.ds(l, cols, stride=levels), :] * factor
                data[slot, l * cols : (l + 1) * cols, 128 * h : 128 * h + 128] = value.astype(BF16)

    for slot in range(own_blocks):
        scale_slot(slot)
    rows_own = data[0:own_blocks].reshape(own_blocks * block_rows, time)
    gram = lax.dot_general(rows_own, rows_own, (((0,), (0,)), ((), ())), preferred_element_type=F32)
    for r in range(rk_n):
        g_local[r] = gram[g_half * r : g_half * (r + 1)]
    wet = jnp.clip(depth_ref[...].astype(F32) - level0, 0.0, float(levels))
    local_count = jnp.broadcast_to(jnp.sum(wet, keepdims=True), (1, time))

    pl.semaphore_wait(barrier, chips)
    halves = pltpu.make_async_remote_copy(
        src_ref=g_local.at[1 - rk], dst_ref=g_peer, send_sem=core_sem.at[4], recv_sem=core_sem.at[5],
        device_id=partner, device_id_type=MESH)
    halves.start()
    t_copy = pltpu.make_async_remote_copy(
        src_ref=t_ref, dst_ref=t_all.at[rk], send_sem=core_sem.at[0], recv_sem=core_sem.at[1],
        device_id=partner, device_id_type=MESH)
    t_copy.start()
    halves.wait()
    for p in range(OWNERS):
        rows = slice(piece * p, piece * (p + 1))
        mine[p, 0:piece, :] = g_local[rk, rows, :] + g_peer[rows, :]
        mine[p, piece : piece + 1, :] = local_count

    def scatter(target):
        return pltpu.make_async_remote_copy(
            src_ref=mine.at[target % OWNERS], dst_ref=parts.at[me],
            send_sem=send_sem.at[0, target], recv_sem=recv_sem.at[0, me],
            device_id=device(target), device_id_type=MESH)

    def scattered(source):
        return pltpu.make_async_remote_copy(
            src_ref=mine.at[0], dst_ref=parts.at[source],
            send_sem=send_sem.at[0, source], recv_sem=recv_sem.at[0, source],
            device_id=device(source), device_id_type=MESH)

    def spread(target):
        return pltpu.make_async_remote_copy(
            src_ref=all_g.at[rk, me % OWNERS], dst_ref=all_g.at[rk, me % OWNERS],
            send_sem=send_sem.at[1, target], recv_sem=recv_sem.at[1, me],
            device_id=device(target), device_id_type=MESH)

    def spreaded(source):
        return pltpu.make_async_remote_copy(
            src_ref=all_g.at[rk, source % OWNERS], dst_ref=all_g.at[rk, source % OWNERS],
            send_sem=send_sem.at[1, source], recv_sem=recv_sem.at[1, source],
            device_id=device(source), device_id_type=MESH)

    each_other(lambda chip: if_owner(chip, lambda: scatter(chip).start()))
    def scale_rest(slot, carry):
        scale_slot(slot)
        return carry

    lax.fori_loop(own_blocks, blocks, scale_rest, 0)

    def reduce():
        parts[me] = mine[me % OWNERS]
        each_other(lambda chip: scattered(chip).wait_recv())
        all_g[rk, me % OWNERS] = jnp.sum(parts[...], axis=0)
        each_other(lambda chip: spread(chip).start())

    if_owner(me, reduce)
    t_copy.wait()
    each_other(lambda chip: if_owner(chip, lambda: scatter(chip).wait_send()))
    each_other(lambda chip: if_owner(chip, lambda: spreaded(chip).wait_recv()))
    swap = pltpu.make_async_remote_copy(
        src_ref=all_g.at[rk], dst_ref=all_g.at[rk], send_sem=core_sem.at[2], recv_sem=core_sem.at[3],
        device_id=partner, device_id_type=MESH)
    swap.start()
    if_owner(me, lambda: each_other(lambda chip: spread(chip).wait_send()))
    test = t_all[...].reshape(rank, time)
    swap.wait()

    whole = all_g[:, :, 0:piece, :].reshape(time, time)
    count = all_g[0, 0, piece : piece + 1, :]
    high = whole.astype(BF16)
    remainder = whole - high.astype(F32)
    middle = remainder.astype(BF16)
    g_parts[0] = high
    g_parts[1] = middle
    g_parts[2] = (remainder - middle.astype(F32)).astype(BF16)

    def times_g(left):
        products = [jnp.dot(left, g_parts[i], preferred_element_type=F32) for i in range(3)]
        return products[0] + (products[1] + products[2])

    z = times_g(test)
    gram0 = sum_parts(dot_last(exact_parts(z), test), rank)
    forward_eliminate(gram0, [z], [solved])
    timerank = solved[...].astype(BF16)

    w = times_g(timerank)
    gram1 = sum_parts(dot_last(exact_parts(w), timerank), rank)
    forward_eliminate(gram1, [w, timerank.astype(F32)], [solved, solved_t])
    root_count = jnp.sqrt(count)
    own = pl.ds(pl.multiple_of(rk * half, half), half)
    coef_ref[...] = solved[own, :] / root_count
    pattern = exact_parts(solved_t[own, :] * root_count)

    def emit(slot, carry):
        e = sum_parts(dot_last(pattern, data[slot]), half)
        block = block_of(slot)
        for l in range(levels):
            eof_ref[block, l] = e[:, l * cols : (l + 1) * cols]
        return carry

    lax.fori_loop(0, blocks, emit, 0, unroll=True)


def local(space_n, lev_n, rk_n, anomaly, depth, cell_weight, test_matrix):
    blocks, cols, levels, time = anomaly.shape
    half = test_matrix.shape[1]
    rank = rk_n * half
    chips = space_n * lev_n
    piece = (time // (rk_n * OWNERS) + 1, time)
    vmem = pl.BlockSpec(memory_space=pltpu.VMEM)
    eof, coefficients = pl.pallas_call(
        functools.partial(kernel, space_n, lev_n, rk_n),
        out_shape=(pltpu.VMEM((blocks, levels, half, cols), F32), pltpu.VMEM((half, time), F32)),
        in_specs=[pl.BlockSpec(memory_space=pltpu.HBM)] * 4,
        out_specs=(vmem, vmem),
        scratch_shapes=[
            pltpu.VMEM((blocks, cols), depth.dtype),
            pltpu.VMEM((blocks, cols), F32),
            pltpu.VMEM((half, time), BF16),
            pltpu.VMEM((blocks, cols * levels, time), BF16),
            pltpu.VMEM((2, time // 128, cols * levels, 128), F32),
            pltpu.VMEM((blocks, cols * levels, time), BF16),
            pltpu.VMEM((rk_n, half, time), BF16),
            pltpu.VMEM((rk_n, time // rk_n, time), F32),
            pltpu.VMEM((time // rk_n, time), F32),
            pltpu.VMEM((OWNERS, *piece), F32),
            pltpu.VMEM((chips, *piece), F32),
            pltpu.VMEM((rk_n, OWNERS, *piece), F32),
            pltpu.VMEM((3, time, time), BF16),
            pltpu.VMEM((rank, time), F32),
            pltpu.VMEM((rank, time), F32),
            pltpu.SemaphoreType.DMA((3,)),
            pltpu.SemaphoreType.DMA((blocks,)),
            pltpu.SemaphoreType.DMA((6,)),
            pltpu.SemaphoreType.DMA((2, chips)),
            pltpu.SemaphoreType.DMA((2, chips)),
        ],
        compiler_params=pltpu.CompilerParams(
            collective_id=0, has_side_effects=True, vmem_limit_bytes=60 * 1024 * 1024),
        name="eof_power_pass",
    )(anomaly.reshape(blocks, cols * levels, time), depth, cell_weight, test_matrix.T)
    return eof.transpose(0, 3, 1, 2), coefficients


def solution(mesh):
    placed = (
        P(("grp", "space"), None, "lev", None),
        P(("grp", "space"), None),
        P(("grp", "space"), None),
        P(None, "rk"),
    )
    sizes = [mesh.shape[axis] for axis in ("space", "lev", "rk")]
    return jax.shard_map(
        functools.partial(local, *sizes),
        mesh=mesh,
        in_specs=placed,
        out_specs=(P(("grp", "space"), None, "lev", "rk"), P(("grp", "rk"), None)),
        check_vma=False,
    )
```

```python
import functools

import jax
import jax.numpy as jnp
from jax import lax
from jax.experimental import pallas as pl
from jax.experimental.pallas import tpu as pltpu
from jax.sharding import PartitionSpec as P

MESH = pl.DeviceIdType.MESH
F32 = jnp.float32
BF16 = jnp.bfloat16
OWNERS = 8
LAST = (((1,), (1,)), ((), ()))


def exact_parts(values):
    high = values.astype(BF16)
    remainder = values - high.astype(F32)
    middle = remainder.astype(BF16)
    lowest = (remainder - middle.astype(F32)).astype(BF16)
    return jnp.concatenate([high, middle, lowest], axis=0)


def sum_parts(stacked, width):
    return stacked[:width] + stacked[width : 2 * width] + stacked[2 * width :]


def dot_last(left, right):
    return lax.dot_general(left, right, LAST, preferred_element_type=F32)


def forward_eliminate(gram, sides, outs):
    rank = gram.shape[0]
    groups = rank // 8
    cols = []
    for g in range(groups):
        cols.append([jnp.broadcast_to(gram[8 * g :, c : c + 1], (rank - 8 * g, 128)) for c in range(8 * g, 8 * g + 8)])
    sides = [list(jnp.split(side, groups, axis=0)) for side in sides]
    rows = lax.broadcasted_iota(jnp.int32, (8, 128), 0)
    for k in range(rank):
        g, at = divmod(k, 8)
        column = cols[g][at]
        pivot = jnp.broadcast_to(column[at : at + 1, :], (8, 128))
        scale = lax.rsqrt(pivot)
        scale = scale * (1.5 - 0.5 * pivot * scale * scale)
        lower = []
        for i in range(g, groups):
            piece = column[8 * (i - g) : 8 * (i - g) + 8] * scale
            if i == g:
                piece = jnp.where(rows > at, piece, 0.0)
            lower.append(piece)
        for side, out in zip(sides, outs):
            width = side[0].shape[1]
            row = side[g][at : at + 1, :] * jnp.concatenate([scale[:1]] * (width // 128), axis=1)
            out[k : k + 1, :] = row
            for i in range(g, groups):
                side[i] = side[i] - jnp.concatenate([lower[i - g]] * (width // 128), axis=1) * row
        for i in range(g, groups):
            tall = lower[i - g] if i == groups - 1 else jnp.concatenate(lower[i - g :], axis=0)
            for c in range(8):
                if 8 * i + c > k:
                    cols[i][c] = cols[i][c] - tall * lower[i - g][c : c + 1, :]


def kernel(space_n, lev_n, rk_n, x_hbm, depth_hbm, weight_hbm, t_hbm, eof_ref, coef_ref,
           depth_ref, weight_ref, t_ref, x_buf, xf, data, t_all, g_local, g_peer, mine, parts, all_g, whole_g, g_parts,
           solved, solved_t, small_sem, in_sem, core_sem, send_sem, recv_sem):
    chips = space_n * lev_n
    blocks, block_rows, time = x_hbm.shape
    cols = depth_ref.shape[1]
    levels = block_rows // cols
    half = t_ref.shape[0]
    rank = rk_n * half
    g_half = time // rk_n
    g_part = g_half // rk_n
    piece, strip = g_half // OWNERS, g_part // OWNERS
    tall = piece + strip
    space, lev, rk = lax.axis_index("space"), lax.axis_index("lev"), lax.axis_index("rk")
    me = space * lev_n + lev
    partner = {"rk": 1 - rk}

    def device(chip):
        return {"space": chip // lev_n, "lev": chip % lev_n}

    def each_other(body):
        if chips <= 16:
            for step in range(1, chips):
                body((me + step) % chips)
        else:
            @pl.loop(1, chips)
            def _(step):
                body((me + step) % chips)

    def if_owner(chip, body):
        body() if chips == OWNERS else pl.when(chip < OWNERS)(body)

    own_blocks = blocks // rk_n

    def block_of(slot):
        return (rk * own_blocks + slot) % blocks

    def load(slot):
        return pltpu.make_async_copy(x_hbm.at[block_of(slot)], x_buf.at[slot], in_sem.at[slot])

    smalls = [
        pltpu.make_async_copy(source, target, small_sem.at[i])
        for i, (source, target) in enumerate(((t_hbm, t_ref), (weight_hbm, weight_ref), (depth_hbm, depth_ref)))
    ]
    load(0).start()
    for small in smalls:
        small.start()
    for slot in range(1, own_blocks):
        load(slot).start()

    barrier = pltpu.get_barrier_semaphore()
    pl.semaphore_signal(barrier, inc=1, device_id=partner, device_id_type=MESH)
    each_other(lambda chip: pl.semaphore_signal(barrier, inc=1, device_id=device(chip), device_id_type=MESH))

    for slot in range(own_blocks, blocks):
        load(slot).start()

    for small in smalls:
        small.wait()
    t_all[rk] = t_ref[...]
    level0 = (lev * levels).astype(F32)

    def scale_slot(slot):
        block = block_of(slot)
        load(slot).wait()
        root = jnp.broadcast_to(jnp.sqrt(weight_ref[pl.ds(block, 1), :]), (128, cols)).T
        deep = jnp.broadcast_to(depth_ref[pl.ds(block, 1), :].astype(F32), (128, cols)).T
        for h in range(time // 128):
            xf[slot % 2, h] = x_buf[slot, :, 128 * h : 128 * h + 128].astype(F32)
        for l in range(levels):
            factor = jnp.where(level0 + l < deep, root, 0.0)
            for h in range(time // 128):
                value = xf[slot % 2, h, pl.ds(l, cols, stride=levels), :] * factor
                data[slot, l * cols : (l + 1) * cols, 128 * h : 128 * h + 128] = value.astype(BF16)

    for slot in range(own_blocks):
        scale_slot(slot)
    rows_own = data[0:own_blocks].reshape(own_blocks * block_rows, time)
    gram = lax.dot_general(rows_own, rows_own, (((0,), (0,)), ((), ())), preferred_element_type=F32)
    for r in range(rk_n):
        for p in range(OWNERS):
            top, side = g_half * r + piece * p, g_part * r + strip * p
            g_local[r, p, 0:piece, :] = gram[top : top + piece, g_half * r : g_half * (r + 1)]
            g_local[r, p, piece:tall, :] = gram[side : side + strip, g_half:]
    wet = jnp.clip(depth_ref[...].astype(F32) - level0, 0.0, float(levels))
    local_count = jnp.broadcast_to(jnp.sum(wet, keepdims=True), (1, g_half))

    pl.semaphore_wait(barrier, chips)
    halves = pltpu.make_async_remote_copy(
        src_ref=g_local.at[1 - rk], dst_ref=g_peer, send_sem=core_sem.at[4], recv_sem=core_sem.at[5],
        device_id=partner, device_id_type=MESH)
    halves.start()
    t_copy = pltpu.make_async_remote_copy(
        src_ref=t_ref, dst_ref=t_all.at[rk], send_sem=core_sem.at[0], recv_sem=core_sem.at[1],
        device_id=partner, device_id_type=MESH)
    t_copy.start()
    halves.wait()
    for p in range(OWNERS):
        mine[p, 0:tall, :] = g_local[rk, p] + g_peer[p]
        mine[p, tall : tall + 1, :] = local_count

    def scatter(target):
        return pltpu.make_async_remote_copy(
            src_ref=mine.at[target % OWNERS], dst_ref=parts.at[me],
            send_sem=send_sem.at[0, target], recv_sem=recv_sem.at[0, me],
            device_id=device(target), device_id_type=MESH)

    def scattered(source):
        return pltpu.make_async_remote_copy(
            src_ref=mine.at[0], dst_ref=parts.at[source],
            send_sem=send_sem.at[0, source], recv_sem=recv_sem.at[0, source],
            device_id=device(source), device_id_type=MESH)

    def spread(target):
        return pltpu.make_async_remote_copy(
            src_ref=all_g.at[rk, me % OWNERS], dst_ref=all_g.at[rk, me % OWNERS],
            send_sem=send_sem.at[1, target], recv_sem=recv_sem.at[1, me],
            device_id=device(target), device_id_type=MESH)

    def spreaded(source):
        return pltpu.make_async_remote_copy(
            src_ref=all_g.at[rk, source % OWNERS], dst_ref=all_g.at[rk, source % OWNERS],
            send_sem=send_sem.at[1, source], recv_sem=recv_sem.at[1, source],
            device_id=device(source), device_id_type=MESH)

    each_other(lambda chip: if_owner(chip, lambda: scatter(chip).start()))
    def scale_rest(slot, carry):
        scale_slot(slot)
        return carry

    lax.fori_loop(own_blocks, blocks, scale_rest, 0)

    def reduce():
        parts[me] = mine[me % OWNERS]
        each_other(lambda chip: scattered(chip).wait_recv())
        all_g[rk, me % OWNERS] = jnp.sum(parts[...], axis=0)
        each_other(lambda chip: spread(chip).start())

    if_owner(me, reduce)
    t_copy.wait()
    each_other(lambda chip: if_owner(chip, lambda: scatter(chip).wait_send()))
    each_other(lambda chip: if_owner(chip, lambda: spreaded(chip).wait_recv()))
    swap = pltpu.make_async_remote_copy(
        src_ref=all_g.at[rk], dst_ref=all_g.at[rk], send_sem=core_sem.at[2], recv_sem=core_sem.at[3],
        device_id=partner, device_id_type=MESH)
    swap.start()
    if_owner(me, lambda: each_other(lambda chip: spread(chip).wait_send()))
    test = t_all[...].reshape(rank, time)
    swap.wait()

    for r in range(rk_n):
        for p in range(OWNERS):
            top, side = g_half * r + piece * p, g_part * r + strip * p
            whole_g[top : top + piece, g_half * r : g_half * (r + 1)] = all_g[r, p, 0:piece, :]
            whole_g[side : side + strip, g_half:] = all_g[r, p, piece:tall, :]
    whole_g[g_half:, 0:g_half] = whole_g[0:g_half, g_half:].T
    whole = whole_g[...]
    count = jnp.concatenate([all_g[0, 0, tall : tall + 1, :]] * rk_n, axis=1)
    high = whole.astype(BF16)
    remainder = whole - high.astype(F32)
    middle = remainder.astype(BF16)
    g_parts[0] = high
    g_parts[1] = middle
    g_parts[2] = (remainder - middle.astype(F32)).astype(BF16)

    def times_g(left):
        products = [jnp.dot(left, g_parts[i], preferred_element_type=F32) for i in range(3)]
        return products[0] + (products[1] + products[2])

    z = times_g(test)
    gram0 = sum_parts(dot_last(exact_parts(z), test), rank)
    forward_eliminate(gram0, [z], [solved])
    timerank = solved[...].astype(BF16)

    w = times_g(timerank)
    gram1 = sum_parts(dot_last(exact_parts(w), timerank), rank)
    forward_eliminate(gram1, [w, timerank.astype(F32)], [solved, solved_t])
    root_count = jnp.sqrt(count)
    own = pl.ds(pl.multiple_of(rk * half, half), half)
    coef_ref[...] = solved[own, :] / root_count
    pattern = exact_parts(solved_t[own, :] * root_count)

    def emit(slot, carry):
        e = sum_parts(dot_last(pattern, data[slot]), half)
        block = block_of(slot)
        for l in range(levels):
            eof_ref[block, l] = e[:, l * cols : (l + 1) * cols]
        return carry

    lax.fori_loop(0, blocks, emit, 0, unroll=True)


def local(space_n, lev_n, rk_n, anomaly, depth, cell_weight, test_matrix):
    blocks, cols, levels, time = anomaly.shape
    half = test_matrix.shape[1]
    rank = rk_n * half
    chips = space_n * lev_n
    g_half = time // rk_n
    tall = g_half // OWNERS + g_half // (rk_n * OWNERS)
    piece = (tall + 1, g_half)
    vmem = pl.BlockSpec(memory_space=pltpu.VMEM)
    eof, coefficients = pl.pallas_call(
        functools.partial(kernel, space_n, lev_n, rk_n),
        out_shape=(pltpu.VMEM((blocks, levels, half, cols), F32), pltpu.VMEM((half, time), F32)),
        in_specs=[pl.BlockSpec(memory_space=pltpu.HBM)] * 4,
        out_specs=(vmem, vmem),
        scratch_shapes=[
            pltpu.VMEM((blocks, cols), depth.dtype),
            pltpu.VMEM((blocks, cols), F32),
            pltpu.VMEM((half, time), BF16),
            pltpu.VMEM((blocks, cols * levels, time), BF16),
            pltpu.VMEM((2, time // 128, cols * levels, 128), F32),
            pltpu.VMEM((blocks, cols * levels, time), BF16),
            pltpu.VMEM((rk_n, half, time), BF16),
            pltpu.VMEM((rk_n, OWNERS, tall, g_half), F32),
            pltpu.VMEM((OWNERS, tall, g_half), F32),
            pltpu.VMEM((OWNERS, *piece), F32),
            pltpu.VMEM((chips, *piece), F32),
            pltpu.VMEM((rk_n, OWNERS, *piece), F32),
            pltpu.VMEM((time, time), F32),
            pltpu.VMEM((3, time, time), BF16),
            pltpu.VMEM((rank, time), F32),
            pltpu.VMEM((rank, time), F32),
            pltpu.SemaphoreType.DMA((3,)),
            pltpu.SemaphoreType.DMA((blocks,)),
            pltpu.SemaphoreType.DMA((6,)),
            pltpu.SemaphoreType.DMA((2, chips)),
            pltpu.SemaphoreType.DMA((2, chips)),
        ],
        compiler_params=pltpu.CompilerParams(
            collective_id=0, has_side_effects=True, vmem_limit_bytes=60 * 1024 * 1024),
        name="eof_power_pass",
    )(anomaly.reshape(blocks, cols * levels, time), depth, cell_weight, test_matrix.T)
    return eof.transpose(0, 3, 1, 2), coefficients


def solution(mesh):
    placed = (
        P(("grp", "space"), None, "lev", None),
        P(("grp", "space"), None),
        P(("grp", "space"), None),
        P(None, "rk"),
    )
    sizes = [mesh.shape[axis] for axis in ("space", "lev", "rk")]
    return jax.shard_map(
        functools.partial(local, *sizes),
        mesh=mesh,
        in_specs=placed,
        out_specs=(P(("grp", "space"), None, "lev", "rk"), P(("grp", "rk"), None)),
        check_vma=False,
    )
```
